32 devices in a mesh: parts: 2 (over y), owner: 16 (over z, x, core).
Axes of the slice: x: 2, y: 2, z: 4, core: 2. Of those that a mesh axis runs over, the one named last changes fastest.
Arguments:
- embeds: bfloat16 [8192, 1024], P(('parts', 'owner')), parts along dimension 0
- cluster: int32 [8192], P(('parts', 'owner')), parts along dimension 0, may hold values from 0 to 63, as said below
- order: int32 [8192], P(('parts', 'owner')), parts along dimension 0, may hold values from 0 to 4095, as said below
Outputs:
- nearest: float32 [8192], P(('parts', 'owner')), parts along dimension 0
The draws below stay inside these ranges and needn't reach their ends.
There are 2 independent parts, one for each index of `parts`. The reference program is written for one: setup_inputs(seed, part) draws one part's arguments, and reference() takes and returns one part's arrays. A program takes and returns all parts, laid end to end along the dimension named above; each array names one. Nothing has to cross between parts.
Inputs may be any that keep to these rules, and one draw needn't show every extreme that they name: Cluster c belongs to owner c // 4. The rows of one device hold at most 32 rows of one owner's clusters; in every draw some owner gets exactly 32 from every device. A cluster has at most 128 rows, and some cluster has exactly 128. `order`: each value occurs once.
All inputs are finite; a program needn't handle non-finite values.
Results may differ from the reference program's by a relative error of at most 0.0003.
Values may be sent and summed in bfloat16 or wider, within the bound.
No kernel may reach another device: no remote copies, remote signals or barrier semaphores. Data moves between devices by JAX's collectives and lax.ppermute only.
A program may use at most 64 MiB of HBM per device.

```python
import jax
import jax.numpy as jnp
from jax import lax

D = 1024
ROWS_DEV = 256
CL_DEV = 4
ROWS = 4096
MEMB = 128


def routing(key):
    ndevs = ROWS // ROWS_DEV
    cap = 2 * ROWS_DEV // ndevs
    busy = jax.random.randint(jax.random.fold_in(key, 21), (), 0, ndevs)

    def one_source(src_key):
        picks = jax.random.permutation(src_key, (ndevs - 1) * cap)[:ROWS_DEV - cap]
        other = (picks // cap).astype(jnp.int32)
        other = other + (other >= busy).astype(jnp.int32)
        dest = jnp.concatenate([jnp.full((cap,), busy, jnp.int32), other])
        return dest[jax.random.permutation(jax.random.fold_in(src_key, 1), ROWS_DEV)]
    dest = jax.vmap(one_source)(jax.random.split(jax.random.fold_in(key, 22), ndevs)).reshape(ROWS)
    sorted_idx = jnp.argsort(dest, stable=True)
    position = jnp.zeros((ROWS,), jnp.int32).at[sorted_idx].set(jnp.arange(ROWS, dtype=jnp.int32))
    counts = jax.ops.segment_sum(jnp.ones((ROWS,), jnp.int32), dest, ndevs)
    start = jnp.cumsum(counts) - counts
    rank = position - start[dest]
    offset = jax.random.randint(jax.random.fold_in(key, 23), (ndevs,), 0, CL_DEV)
    return (dest * CL_DEV + (rank + offset[dest]) % CL_DEV).astype(jnp.int32)


def draw_cluster(key, part):
    return routing(key)


def draw_embeds(key, part):
    labels = routing(key)
    key = jax.random.fold_in(key, 5)
    centre_key = jax.random.fold_in(key, 1)
    centres = jax.vmap(lambda c: jax.random.normal(jax.random.fold_in(centre_key, c), (D,), jnp.float32))(labels)
    amplitude = jnp.exp(jax.random.uniform(jax.random.fold_in(key, 2), (ROWS, 1), jnp.float32, jnp.log(0.3), jnp.log(3.0)))
    noise = jax.random.normal(jax.random.fold_in(key, 3), (ROWS, D), jnp.float32)
    values = amplitude * centres + noise
    return values.astype(jnp.bfloat16)


def draw_order(key, part):
    key = jax.random.fold_in(key, 7)
    return jax.random.permutation(key, ROWS).astype(jnp.int32)


def setup_inputs(seed: int = 0, part: int = 0) -> dict:
    splits = jax.random.split(jax.random.key(seed), 4)
    part_splits = jax.random.split(jax.random.fold_in(splits[3], part), 4)
    embeds = draw_embeds(jax.random.fold_in(jax.random.fold_in(splits[3], part), 71), part)
    cluster = draw_cluster(jax.random.fold_in(jax.random.fold_in(splits[3], part), 71), part)
    order = draw_order(jax.random.fold_in(jax.random.fold_in(splits[3], part), 71), part)
    return {"embeds": embeds, "cluster": cluster, "order": order}


def reference(embeds, cluster, order):
    perm = jnp.argsort(cluster, stable=True)
    rows = embeds[perm].astype(jnp.float32)
    labels = cluster[perm]
    orders = order[perm]
    scale = lax.rsqrt(lax.optimization_barrier(jnp.mean(rows * rows, axis=1)) + 1e-06)
    count = rows.shape[0]
    block = min(512, count)
    nblocks = count // block
    reach = MEMB
    rows_pad = jnp.pad(rows, ((reach, reach), (0, 0)))
    scale_pad = jnp.pad(scale, (reach, reach))
    labels_pad = jnp.pad(labels, (reach, reach), constant_values=-2)
    orders_pad = jnp.pad(orders, (reach, reach))

    def one_tile(index):
        start = (index * block).astype(jnp.int32)
        rows_blk = lax.dynamic_slice_in_dim(rows, start, block, 0)
        scale_blk = lax.dynamic_slice_in_dim(scale, start, block, 0)
        label_blk = lax.dynamic_slice_in_dim(labels, start, block, 0)
        order_blk = lax.dynamic_slice_in_dim(orders, start, block, 0)
        window = lax.dynamic_slice_in_dim(rows_pad, start, block + 2 * reach, 0)
        scale_win = lax.dynamic_slice_in_dim(scale_pad, start, block + 2 * reach, 0)
        label_win = lax.dynamic_slice_in_dim(labels_pad, start, block + 2 * reach, 0)
        order_win = lax.dynamic_slice_in_dim(orders_pad, start, block + 2 * reach, 0)
        gram = jnp.dot(rows_blk, window.T, precision=lax.Precision.HIGHEST)
        cosine = gram * scale_blk[:, None] * scale_win[None, :] / D
        usable = (label_blk[:, None] == label_win[None, :]) & (order_win[None, :] < order_blk[:, None])
        return lax.optimization_barrier(jnp.max(jnp.where(usable, cosine, -1.0), axis=1))
    best = lax.map(one_tile, jnp.arange(nblocks, dtype=jnp.int32)).reshape(count)
    return jnp.zeros((count,), jnp.float32).at[perm].set(best)
```

```python
import functools

import jax
import jax.numpy as jnp
from jax import lax
from jax.experimental import pallas as pl
from jax.experimental.pallas import tpu as pltpu
from jax.sharding import PartitionSpec as P

CL_DEV = 4
LANES = 128
EMPTY = 1e9
NOBODY = 2e9
LOWEST = -3e38
STEP = 65536.0


def iota(shape, dim):
    return lax.broadcasted_iota(jnp.int32, shape, dim)


def nt(a, b):
    return lax.dot_general(a, b, (((1,), (1,)), ((), ())), preferred_element_type=jnp.float32)


def nn(a, b):
    return lax.dot_general(a, b, (((1,), (0,)), ((), ())), preferred_element_type=jnp.float32)


def pack_kernel(peers, rows, cap, shift, cl_ref, od_ref, x_ref, out_ref, route_ref):
    count = x_ref.shape[0]
    cl = cl_ref[...]
    od = od_ref[...]
    dest = cl >> shift
    group = cl & (2**shift - 1)
    mine = iota((peers, count), 0) == dest
    before = (iota((count, count), 0) < iota((count, count), 1)).astype(jnp.bfloat16)
    ahead = nn(mine.astype(jnp.bfloat16), before)
    rank = jnp.sum(jnp.where(mine, ahead, 0.0), axis=0, keepdims=True).astype(jnp.int32)
    route_ref[0:1, :] = dest
    route_ref[1:2, :] = rank
    fits = rank < cap
    slot = jnp.where(fits, dest * rows + rank, -1)
    pick = (iota((peers * rows, count), 0) == slot).astype(jnp.bfloat16)
    fields = [od >> 8, od & 255, group + 1]
    spread = jnp.concatenate(
        [jnp.where(mine, f.astype(jnp.float32), 0.0) for f in fields], axis=0
    ).astype(jnp.bfloat16)
    place = ((iota((LANES, count), 0) == rank) & fits).astype(jnp.bfloat16)
    tags = nt(spread, place).astype(jnp.bfloat16)
    tag_row = (iota((peers * rows, peers), 0) == iota((peers * rows, peers), 1) * rows + cap).astype(jnp.bfloat16)
    width = x_ref.shape[1]
    step = 2 * LANES
    for k in range(width // step):
        part = nn(pick, x_ref[:, k * step:(k + 1) * step])
        if k == 0:
            part += nn(tag_row, jnp.concatenate([tags[0:peers], tags[peers:2 * peers]], axis=1))
        if k == 1:
            part += nn(tag_row, jnp.concatenate([tags[2 * peers:], jnp.zeros((peers, LANES), jnp.bfloat16)], axis=1))
        out_ref[:, k * step:(k + 1) * step] = part.astype(jnp.bfloat16)


def best_kernel(peers, rows, cap, x_ref, best_ref):
    total, width = x_ref.shape
    gram = nt(x_ref[...], x_ref[...])
    tag_row = (iota((peers, total), 1) == iota((peers, total), 0) * rows + cap).astype(jnp.bfloat16)
    tags = nn(tag_row, x_ref[:, :4 * LANES])
    cols = iota((peers, total), 1)
    first = iota((peers, total), 0) * rows
    block = (cols >= first) & (cols < first + rows)
    position = jnp.sum(jnp.where(block, cols - first, 0), axis=0, keepdims=True)
    spread = (iota((LANES, total), 0) == position).astype(jnp.bfloat16)
    fields = jnp.concatenate([tags[:, f * LANES:(f + 1) * LANES] for f in range(3)], axis=0).astype(jnp.bfloat16)
    flat = nn(fields, spread)
    high, low, group = [
        jnp.sum(jnp.where(block, flat[f * peers:(f + 1) * peers], 0.0), axis=0, keepdims=True) for f in range(3)
    ]
    filled = group > 0.5
    key = jnp.where(filled, group * STEP + high * 256.0 + low, EMPTY)
    floor = jnp.where(filled, group * STEP, NOBODY)
    eye = iota((total, total), 0) == iota((total, total), 1)
    key_col = jnp.sum(jnp.where(eye, key, 0.0), axis=1, keepdims=True)
    diagonal = jnp.where(eye, gram, 0.0)
    scale = lax.rsqrt(jnp.sum(diagonal, axis=0, keepdims=True) / width + 1e-06)
    scale_col = lax.rsqrt(jnp.sum(diagonal, axis=1, keepdims=True) / width + 1e-06)
    usable = (key_col < key) & (key_col >= floor)
    largest = jnp.max(jnp.where(usable, gram * scale_col, LOWEST), axis=0, keepdims=True)
    best = jnp.where(largest > LOWEST, jnp.maximum(largest * scale / width, -1.0), -1.0)
    best_ref[...] = jnp.broadcast_to(best, best_ref.shape)


def take_kernel(rows, me_ref, best_ref, route_ref, out_ref):
    peers, total = best_ref.shape
    count = out_ref.shape[1]
    dest = route_ref[0:1, :]
    slot = me_ref[0] * rows + route_ref[1:2, :]
    best = best_ref[...]
    high = best.astype(jnp.bfloat16)
    rest = best - high.astype(jnp.float32)
    mid = rest.astype(jnp.bfloat16)
    low = (rest - mid.astype(jnp.float32)).astype(jnp.bfloat16)
    pick = (iota((total, count), 0) == slot).astype(jnp.bfloat16)
    found = nn(high, pick) + nn(mid, pick) + nn(low, pick)
    mine = iota((peers, count), 0) == dest
    out_ref[...] = jnp.sum(jnp.where(mine, found, 0.0), axis=0, keepdims=True)


def per_device(embeds, cluster, order):
    count, width = embeds.shape
    peers = lax.axis_size("owner")
    cap = 2 * count // peers
    rows = -(-(cap + 1) // 8) * 8
    total = peers * rows
    shift = CL_DEV.bit_length() - 1
    vmem = pl.BlockSpec(memory_space=pltpu.VMEM)
    smem = pl.BlockSpec(memory_space=pltpu.SMEM)
    params = pltpu.CompilerParams(vmem_limit_bytes=48 * 2**20)
    packed, route = pl.pallas_call(
        functools.partial(pack_kernel, peers, rows, cap, shift),
        out_shape=[
            jax.ShapeDtypeStruct((total, width), jnp.bfloat16),
            jax.ShapeDtypeStruct((2, count), jnp.int32),
        ],
        in_specs=[vmem] * 3,
        out_specs=[vmem] * 2,
        compiler_params=params,
    )(cluster.reshape(1, count), order.reshape(1, count), embeds)
    arrived = lax.all_to_all(packed.reshape(peers, rows, width), "owner", split_axis=0, concat_axis=0, tiled=True)
    best = pl.pallas_call(
        functools.partial(best_kernel, peers, rows, cap),
        out_shape=jax.ShapeDtypeStruct((peers, total), jnp.float32),
        in_specs=[vmem],
        out_specs=vmem,
        compiler_params=params,
    )(arrived.reshape(total, width))
    returned = lax.all_to_all(best, "owner", split_axis=0, concat_axis=0, tiled=True)
    me = lax.axis_index("owner").astype(jnp.int32).reshape(1)
    nearest = pl.pallas_call(
        functools.partial(take_kernel, rows),
        out_shape=jax.ShapeDtypeStruct((1, count), jnp.float32),
        in_specs=[smem, vmem, vmem],
        out_specs=vmem,
        compiler_params=params,
    )(me, returned, route)
    return nearest.reshape(count)


def solution(mesh):
    placed = (P(("parts", "owner"), None), P(("parts", "owner")), P(("parts", "owner")))
    return jax.shard_map(
        per_device, mesh=mesh, in_specs=placed, out_specs=P(("parts", "owner")), check_vma=False
    )
```

```python
import functools

import jax
import jax.numpy as jnp
from jax import lax
from jax.experimental import pallas as pl
from jax.experimental.pallas import tpu as pltpu
from jax.sharding import PartitionSpec as P

CL_DEV = 4
LANES = 128
EMPTY = 1e9
NOBODY = 2e9
LOWEST = -3e38
STEP = 65536.0
PARAMS = pltpu.CompilerParams(vmem_limit_bytes=48 * 2**20)


def iota(shape, dim):
    return lax.broadcasted_iota(jnp.int32, shape, dim)


def nt(a, b):
    return lax.dot_general(a, b, (((1,), (1,)), ((), ())), preferred_element_type=jnp.float32)


def nn(a, b):
    return lax.dot_general(a, b, (((1,), (0,)), ((), ())), preferred_element_type=jnp.float32)


def pack_kernel(peers, rows, cap, spread_out, cl_hbm, od_hbm, x_hbm, out_ref, route_ref, cl_ref, od_ref, x_ref, sems):
    copies = [
        pltpu.make_async_copy(src, dst, sems.at[k])
        for k, (src, dst) in enumerate([(cl_hbm, cl_ref), (od_hbm, od_ref), (x_hbm, x_ref)])
    ]
    for copy in copies:
        copy.start()
    copies[0].wait()
    copies[1].wait()
    count = x_ref.shape[0]
    cl = cl_ref[...]
    od = od_ref[...]
    if spread_out:
        dest = cl & (peers - 1)
        group = cl >> (peers.bit_length() - 1)
    else:
        dest = cl >> (CL_DEV.bit_length() - 1)
        group = cl & (CL_DEV - 1)
    mine = iota((peers, count), 0) == dest
    before = (iota((count, count), 0) < iota((count, count), 1)).astype(jnp.bfloat16)
    ahead = nn(mine.astype(jnp.bfloat16), before)
    rank = jnp.sum(jnp.where(mine, ahead, 0.0), axis=0, keepdims=True).astype(jnp.int32)
    route_ref[0:1, :] = dest
    route_ref[1:2, :] = rank
    fits = rank < cap
    slot = jnp.where(fits, dest * rows + rank, -1)
    pick = (iota((peers * rows, count), 0) == slot).astype(jnp.bfloat16)
    fields = [od >> 8, od & 255, group + 1]
    spread = jnp.concatenate(
        [jnp.where(mine, f.astype(jnp.float32), 0.0) for f in fields], axis=0
    ).astype(jnp.bfloat16)
    place = ((iota((LANES, count), 0) == rank) & fits).astype(jnp.bfloat16)
    tags = nt(spread, place).astype(jnp.bfloat16)
    tag_row = (iota((peers * rows, peers), 0) == iota((peers * rows, peers), 1) * rows + cap).astype(jnp.bfloat16)
    crowded = jnp.max((rank >= cap).astype(jnp.float32), axis=1, keepdims=True)
    crowded = jnp.broadcast_to(crowded, (peers, LANES)).astype(jnp.bfloat16)
    width = x_ref.shape[1]
    step = 2 * LANES
    copies[2].wait()
    for k in range(width // step):
        part = nn(pick, x_ref[:, k * step:(k + 1) * step])
        if k == 0:
            part += nn(tag_row, jnp.concatenate([tags[0:peers], tags[peers:2 * peers]], axis=1))
        if k == 1:
            part += nn(tag_row, jnp.concatenate([tags[2 * peers:], crowded], axis=1))
        out_ref[:, k * step:(k + 1) * step] = part.astype(jnp.bfloat16)


def best_kernel(peers, rows, cap, x_ref, best_ref, crowded_ref):
    total, width = x_ref.shape
    gram = nt(x_ref[...], x_ref[...])
    tag_row = (iota((peers, total), 1) == iota((peers, total), 0) * rows + cap).astype(jnp.bfloat16)
    tags = nn(tag_row, x_ref[:, :4 * LANES])
    crowded_ref[0] = jnp.max(tags[:, 3 * LANES:]).astype(jnp.int32)
    cols = iota((peers, total), 1)
    first = iota((peers, total), 0) * rows
    block = (cols >= first) & (cols < first + rows)
    position = jnp.sum(jnp.where(block, cols - first, 0), axis=0, keepdims=True)
    spread = (iota((LANES, total), 0) == position).astype(jnp.bfloat16)
    fields = jnp.concatenate([tags[:, f * LANES:(f + 1) * LANES] for f in range(3)], axis=0).astype(jnp.bfloat16)
    flat = nn(fields, spread)
    high, low, group = [
        jnp.sum(jnp.where(block, flat[f * peers:(f + 1) * peers], 0.0), axis=0, keepdims=True) for f in range(3)
    ]
    filled = group > 0.5
    key = jnp.where(filled, group * STEP + high * 256.0 + low, EMPTY)
    floor = jnp.where(filled, group * STEP, NOBODY)
    eye = iota((total, total), 0) == iota((total, total), 1)
    key_col = jnp.sum(jnp.where(eye, key, 0.0), axis=1, keepdims=True)
    diagonal = jnp.where(eye, gram, 0.0)
    scale = lax.rsqrt(jnp.sum(diagonal, axis=0, keepdims=True) / width + 1e-06)
    scale_col = lax.rsqrt(jnp.sum(diagonal, axis=1, keepdims=True) / width + 1e-06)
    usable = (key_col < key) & (key_col >= floor)
    largest = jnp.max(jnp.where(usable, gram * scale_col, LOWEST), axis=0, keepdims=True)
    best = jnp.where(largest > LOWEST, jnp.maximum(largest * scale / width, -1.0), -1.0)
    best_ref[...] = jnp.broadcast_to(best, best_ref.shape)


def take_kernel(rows, me_ref, best_ref, route_ref, out_ref):
    peers, total = best_ref.shape
    count = out_ref.shape[1]
    dest = route_ref[0:1, :]
    slot = me_ref[0] * rows + route_ref[1:2, :]
    best = best_ref[...]
    high = best.astype(jnp.bfloat16)
    rest = best - high.astype(jnp.float32)
    mid = rest.astype(jnp.bfloat16)
    low = (rest - mid.astype(jnp.float32)).astype(jnp.bfloat16)
    pick = (iota((total, count), 0) == slot).astype(jnp.bfloat16)
    found = nn(high, pick) + nn(mid, pick) + nn(low, pick)
    mine = iota((peers, count), 0) == dest
    out_ref[...] = jnp.sum(jnp.where(mine, found, 0.0), axis=0, keepdims=True)


def send(rows, cap, spread_out, embeds, cluster, order):
    count, width = embeds.shape
    peers = lax.axis_size("owner")
    total = peers * rows
    vmem = pl.BlockSpec(memory_space=pltpu.VMEM)
    smem = pl.BlockSpec(memory_space=pltpu.SMEM)
    packed, route = pl.pallas_call(
        functools.partial(pack_kernel, peers, rows, cap, spread_out),
        out_shape=[
            jax.ShapeDtypeStruct((total, width), jnp.bfloat16),
            jax.ShapeDtypeStruct((2, count), jnp.int32),
        ],
        in_specs=[pl.BlockSpec(memory_space=pl.ANY)] * 3,
        out_specs=[vmem] * 2,
        scratch_shapes=[
            pltpu.VMEM((1, count), jnp.int32),
            pltpu.VMEM((1, count), jnp.int32),
            pltpu.VMEM((count, width), jnp.bfloat16),
            pltpu.SemaphoreType.DMA((3,)),
        ],
        compiler_params=PARAMS,
    )(cluster.reshape(1, count), order.reshape(1, count), embeds)
    arrived = lax.all_to_all(packed.reshape(peers, rows, width), "owner", split_axis=0, concat_axis=0, tiled=True)
    best, crowded = pl.pallas_call(
        functools.partial(best_kernel, peers, rows, cap),
        out_shape=[jax.ShapeDtypeStruct((peers, total), jnp.float32), jax.ShapeDtypeStruct((1,), jnp.int32)],
        in_specs=[vmem],
        out_specs=[vmem, smem],
        compiler_params=PARAMS,
    )(arrived.reshape(total, width))
    return best, route, crowded


def bring_back(rows, best, route):
    count = route.shape[1]
    vmem = pl.BlockSpec(memory_space=pltpu.VMEM)
    smem = pl.BlockSpec(memory_space=pltpu.SMEM)
    returned = lax.all_to_all(best, "owner", split_axis=0, concat_axis=0, tiled=True)
    me = lax.axis_index("owner").astype(jnp.int32).reshape(1)
    nearest = pl.pallas_call(
        functools.partial(take_kernel, rows),
        out_shape=jax.ShapeDtypeStruct((1, count), jnp.float32),
        in_specs=[smem, vmem, vmem],
        out_specs=vmem,
        compiler_params=PARAMS,
    )(me, returned, route)
    return nearest.reshape(count)


def per_device(embeds, cluster, order):
    count = embeds.shape[0]
    most = 2 * count // lax.axis_size("owner")

    def roomy(embeds, cluster, order):
        rows = -(-(most + 1) // 8) * 8
        best, route, _ = send(rows, most, False, embeds, cluster, order)
        return bring_back(rows, best, route)

    rows = 3 * most // 4
    if rows % 8:
        return roomy(embeds, cluster, order)
    best, route, crowded = send(rows, rows - 1, True, embeds, cluster, order)
    return lax.cond(
        crowded[0] > 0,
        lambda: roomy(embeds, cluster, order),
        lambda: bring_back(rows, best, route),
    )


def solution(mesh):
    placed = (P(("parts", "owner"), None), P(("parts", "owner")), P(("parts", "owner")))
    return jax.shard_map(
        per_device, mesh=mesh, in_specs=placed, out_specs=P(("parts", "owner")), check_vma=False
    )
```

```python
import functools

import jax
import jax.numpy as jnp
from jax import lax
from jax.experimental import pallas as pl
from jax.experimental.pallas import tpu as pltpu
from jax.sharding import PartitionSpec as P

CL_DEV = 4
LANES = 128
EMPTY = 1e9
NOBODY = 2e9
LOWEST = -3e38
STEP = 65536.0
PARAMS = pltpu.CompilerParams(vmem_limit_bytes=48 * 2**20)


def iota(shape, dim):
    return lax.broadcasted_iota(jnp.int32, shape, dim)


def nt(a, b):
    return lax.dot_general(a, b, (((1,), (1,)), ((), ())), preferred_element_type=jnp.float32)


def nn(a, b):
    return lax.dot_general(a, b, (((1,), (0,)), ((), ())), preferred_element_type=jnp.float32)


def pack_kernel(peers, rows, cap, spread_out, cl_hbm, od_hbm, x_hbm, out_ref, route_ref, cl_ref, od_ref, x_ref, sems):
    count, width = x_ref.shape
    step = 2 * LANES
    pieces = [(cl_hbm, cl_ref), (od_hbm, od_ref)]
    for k in range(width // step):
        columns = pl.ds(k * step, step)
        pieces.append((x_hbm.at[:, columns], x_ref.at[:, columns]))
    copies = [pltpu.make_async_copy(src, dst, sems.at[k]) for k, (src, dst) in enumerate(pieces)]
    for copy in copies:
        copy.start()
    copies[0].wait()
    copies[1].wait()
    cl = cl_ref[...]
    od = od_ref[...]
    if spread_out:
        dest = cl & (peers - 1)
        group = cl >> (peers.bit_length() - 1)
    else:
        dest = cl >> (CL_DEV.bit_length() - 1)
        group = cl & (CL_DEV - 1)
    mine = iota((peers, count), 0) == dest
    before = (iota((count, count), 0) < iota((count, count), 1)).astype(jnp.bfloat16)
    ahead = nn(mine.astype(jnp.bfloat16), before)
    rank = jnp.sum(jnp.where(mine, ahead, 0.0), axis=0, keepdims=True).astype(jnp.int32)
    route_ref[0:1, :] = dest
    route_ref[1:2, :] = rank
    fits = rank < cap
    slot = jnp.where(fits, dest * rows + rank, -1)
    pick = (iota((peers * rows, count), 0) == slot).astype(jnp.bfloat16)
    fields = [od >> 8, od & 255, group + 1]
    spread = jnp.concatenate(
        [jnp.where(mine, f.astype(jnp.float32), 0.0) for f in fields], axis=0
    ).astype(jnp.bfloat16)
    place = ((iota((LANES, count), 0) == rank) & fits).astype(jnp.bfloat16)
    tags = nt(spread, place).astype(jnp.bfloat16)
    tag_row = (iota((peers * rows, peers), 0) == iota((peers * rows, peers), 1) * rows + cap).astype(jnp.bfloat16)
    crowded = jnp.max((rank >= cap).astype(jnp.float32), axis=1, keepdims=True)
    crowded = jnp.broadcast_to(crowded, (peers, LANES)).astype(jnp.bfloat16)
    for k in range(width // step):
        copies[2 + k].wait()
        part = nn(pick, x_ref[:, k * step:(k + 1) * step])
        if k == 0:
            part += nn(tag_row, jnp.concatenate([tags[0:peers], tags[peers:2 * peers]], axis=1))
        if k == 1:
            part += nn(tag_row, jnp.concatenate([tags[2 * peers:], crowded], axis=1))
        out_ref[:, k * step:(k + 1) * step] = part.astype(jnp.bfloat16)


def best_kernel(peers, rows, cap, x_ref, best_ref, crowded_ref):
    total, width = x_ref.shape
    gram = nt(x_ref[...], x_ref[...])
    tag_row = (iota((peers, total), 1) == iota((peers, total), 0) * rows + cap).astype(jnp.bfloat16)
    tags = nn(tag_row, x_ref[:, :4 * LANES])
    crowded_ref[0] = jnp.max(tags[:, 3 * LANES:]).astype(jnp.int32)
    cols = iota((peers, total), 1)
    first = iota((peers, total), 0) * rows
    block = (cols >= first) & (cols < first + rows)
    position = jnp.sum(jnp.where(block, cols - first, 0), axis=0, keepdims=True)
    spread = (iota((LANES, total), 0) == position).astype(jnp.bfloat16)
    fields = jnp.concatenate([tags[:, f * LANES:(f + 1) * LANES] for f in range(3)], axis=0).astype(jnp.bfloat16)
    flat = nn(fields, spread)
    high, low, group = [
        jnp.sum(jnp.where(block, flat[f * peers:(f + 1) * peers], 0.0), axis=0, keepdims=True) for f in range(3)
    ]
    filled = group > 0.5
    key = jnp.where(filled, group * STEP + high * 256.0 + low, EMPTY)
    floor = jnp.where(filled, group * STEP, NOBODY)
    eye = iota((total, total), 0) == iota((total, total), 1)
    key_col = jnp.sum(jnp.where(eye, key, 0.0), axis=1, keepdims=True)
    diagonal = jnp.where(eye, gram, 0.0)
    scale = lax.rsqrt(jnp.sum(diagonal, axis=0, keepdims=True) / width + 1e-06)
    scale_col = lax.rsqrt(jnp.sum(diagonal, axis=1, keepdims=True) / width + 1e-06)
    usable = (key_col < key) & (key_col >= floor)
    largest = jnp.max(jnp.where(usable, gram * scale_col, LOWEST), axis=0, keepdims=True)
    best = jnp.where(largest > LOWEST, jnp.maximum(largest * scale / width, -1.0), -1.0)
    best_ref[...] = jnp.broadcast_to(best[None], best_ref.shape)


def take_kernel(rows, me_ref, best_ref, route_ref, out_ref):
    peers, _, total = best_ref.shape
    count = out_ref.shape[1]
    dest = route_ref[0:1, :]
    slot = me_ref[0] * rows + route_ref[1:2, :]
    best = best_ref[:, 0, :]
    high = best.astype(jnp.bfloat16)
    rest = best - high.astype(jnp.float32)
    mid = rest.astype(jnp.bfloat16)
    low = (rest - mid.astype(jnp.float32)).astype(jnp.bfloat16)
    pick = (iota((total, count), 0) == slot).astype(jnp.bfloat16)
    found = nn(high, pick) + nn(mid, pick) + nn(low, pick)
    mine = iota((peers, count), 0) == dest
    out_ref[...] = jnp.sum(jnp.where(mine, found, 0.0), axis=0, keepdims=True)


def exchange(blocks):
    peers = blocks.shape[0]
    group = [(k + peers // 2 + 1) % peers for k in range(peers)]
    return lax.all_to_all(blocks, "owner", split_axis=0, concat_axis=0, tiled=True, axis_index_groups=[group])


def place_in_group():
    peers = lax.axis_size("owner")
    return ((lax.axis_index("owner") + (peers - peers // 2 - 1)) % peers).astype(jnp.int32).reshape(1)


def send(rows, cap, spread_out, embeds, cluster, order):
    count, width = embeds.shape
    peers = lax.axis_size("owner")
    total = peers * rows
    vmem = pl.BlockSpec(memory_space=pltpu.VMEM)
    smem = pl.BlockSpec(memory_space=pltpu.SMEM)
    packed, route = pl.pallas_call(
        functools.partial(pack_kernel, peers, rows, cap, spread_out),
        out_shape=[
            jax.ShapeDtypeStruct((total, width), jnp.bfloat16),
            jax.ShapeDtypeStruct((2, count), jnp.int32),
        ],
        in_specs=[pl.BlockSpec(memory_space=pl.ANY)] * 3,
        out_specs=[vmem] * 2,
        scratch_shapes=[
            pltpu.VMEM((1, count), jnp.int32),
            pltpu.VMEM((1, count), jnp.int32),
            pltpu.VMEM((count, width), jnp.bfloat16),
            pltpu.SemaphoreType.DMA((2 + width // (2 * LANES),)),
        ],
        compiler_params=PARAMS,
    )(cluster.reshape(1, count), order.reshape(1, count), embeds)
    arrived = exchange(packed.reshape(peers, rows, width))
    best, crowded = pl.pallas_call(
        functools.partial(best_kernel, peers, rows, cap),
        out_shape=[jax.ShapeDtypeStruct((peers, 1, total), jnp.float32), jax.ShapeDtypeStruct((1,), jnp.int32)],
        in_specs=[vmem],
        out_specs=[vmem, smem],
        compiler_params=PARAMS,
    )(arrived.reshape(total, width))
    return best, route, crowded


def take(rows, me, returned, route):
    count = route.shape[1]
    vmem = pl.BlockSpec(memory_space=pltpu.VMEM)
    smem = pl.BlockSpec(memory_space=pltpu.SMEM)
    nearest = pl.pallas_call(
        functools.partial(take_kernel, rows),
        out_shape=jax.ShapeDtypeStruct((1, count), jnp.float32),
        in_specs=[smem, vmem, vmem],
        out_specs=vmem,
        compiler_params=PARAMS,
    )(me, returned, route)
    return nearest.reshape(count)


def per_device(embeds, cluster, order):
    count = embeds.shape[0]
    most = 2 * count // lax.axis_size("owner")

    def roomy():
        rows = -(-(most + 1) // 8) * 8
        best, route, _ = send(rows, most, False, embeds, cluster, order)
        return take(rows, place_in_group(), exchange(best), route)

    rows = 3 * most // 4
    if rows % 8:
        return roomy()
    best, route, crowded = send(rows, rows - 1, True, embeds, cluster, order)
    returned = exchange(best)

    def again():
        results = jnp.zeros_like(returned).at[0, 0, :count].set(roomy())
        places = jnp.stack([jnp.zeros((count,), jnp.int32), jnp.arange(count, dtype=jnp.int32)])
        return jnp.zeros((1,), jnp.int32), results, places

    return take(rows, *lax.cond(crowded[0] > 0, again, lambda: (place_in_group(), returned, route)))


def solution(mesh):
    placed = (P(("parts", "owner"), None), P(("parts", "owner")), P(("parts", "owner")))
    return jax.shard_map(
        per_device, mesh=mesh, in_specs=placed, out_specs=P(("parts", "owner")), check_vma=False
    )
```

```python
import functools

import jax
import jax.numpy as jnp
from jax import lax
from jax.experimental import pallas as pl
from jax.experimental.pallas import tpu as pltpu
from jax.sharding import PartitionSpec as P

CL_DEV = 4
LANES = 128
EMPTY = 1e9
NOBODY = 2e9
LOWEST = -3e38
STEP = 65536.0
PARAMS = pltpu.CompilerParams(vmem_limit_bytes=48 * 2**20)


def iota(shape, dim):
    return lax.broadcasted_iota(jnp.int32, shape, dim)


def nt(a, b):
    return lax.dot_general(a, b, (((1,), (1,)), ((), ())), preferred_element_type=jnp.float32)


def nn(a, b):
    return lax.dot_general(a, b, (((1,), (0,)), ((), ())), preferred_element_type=jnp.float32)


def pack_kernel(peers, rows, cap, spread_out, cl_hbm, od_hbm, x_hbm, out_ref, route_ref, cl_ref, od_ref, x_ref, sems):
    count, width = x_ref.shape
    step = 2 * LANES
    pieces = [(cl_hbm, cl_ref), (od_hbm, od_ref), (x_hbm, x_ref)]
    copies = [pltpu.make_async_copy(src, dst, sems.at[k]) for k, (src, dst) in enumerate(pieces)]
    for copy in copies:
        copy.start()
    before = (iota((count, count), 0) < iota((count, count), 1)).astype(jnp.bfloat16)
    tag_row = (iota((peers * rows, peers), 0) == iota((peers * rows, peers), 1) * rows + cap).astype(jnp.bfloat16)
    copies[0].wait()
    copies[1].wait()
    cl = cl_ref[...]
    od = od_ref[...]
    if spread_out:
        dest = cl & (peers - 1)
        group = cl >> (peers.bit_length() - 1)
    else:
        dest = cl >> (CL_DEV.bit_length() - 1)
        group = cl & (CL_DEV - 1)
    mine = iota((peers, count), 0) == dest
    ahead = nn(mine.astype(jnp.bfloat16), before)
    rank = jnp.sum(jnp.where(mine, ahead, 0.0), axis=0, keepdims=True).astype(jnp.int32)
    route_ref[0:1, :] = dest
    route_ref[1:2, :] = rank
    fits = rank < cap
    slot = jnp.where(fits, dest * rows + rank, -1)
    pick = (iota((peers * rows, count), 0) == slot).astype(jnp.bfloat16)
    fields = [od >> 8, od & 255, group + 1]
    spread = jnp.concatenate(
        [jnp.where(mine, f.astype(jnp.float32), 0.0) for f in fields], axis=0
    ).astype(jnp.bfloat16)
    place = ((iota((LANES, count), 0) == rank) & fits).astype(jnp.bfloat16)
    tags = nt(spread, place).astype(jnp.bfloat16)
    crowded = jnp.max((rank >= cap).astype(jnp.float32), axis=1, keepdims=True)
    crowded = jnp.broadcast_to(crowded, (peers, LANES)).astype(jnp.bfloat16)
    copies[2].wait()
    for k in range(width // step):
        part = nn(pick, x_ref[:, k * step:(k + 1) * step])
        if k == 0:
            part += nn(tag_row, jnp.concatenate([tags[0:peers], tags[peers:2 * peers]], axis=1))
        if k == 1:
            part += nn(tag_row, jnp.concatenate([tags[2 * peers:], crowded], axis=1))
        out_ref[:, k * step:(k + 1) * step] = part.astype(jnp.bfloat16)


def best_kernel(peers, rows, cap, x_ref, best_ref, crowded_ref):
    total, width = x_ref.shape
    gram = nt(x_ref[...], x_ref[...])
    tag_row = (iota((peers, total), 1) == iota((peers, total), 0) * rows + cap).astype(jnp.bfloat16)
    tags = nn(tag_row, x_ref[:, :4 * LANES])
    crowded_ref[0] = jnp.max(tags[:, 3 * LANES:]).astype(jnp.int32)
    cols = iota((peers, total), 1)
    first = iota((peers, total), 0) * rows
    block = (cols >= first) & (cols < first + rows)
    position = jnp.sum(jnp.where(block, cols - first, 0), axis=0, keepdims=True)
    spread = (iota((LANES, total), 0) == position).astype(jnp.bfloat16)
    fields = jnp.concatenate([tags[:, f * LANES:(f + 1) * LANES] for f in range(3)], axis=0).astype(jnp.bfloat16)
    flat = nn(fields, spread)
    high, low, group = [
        jnp.sum(jnp.where(block, flat[f * peers:(f + 1) * peers], 0.0), axis=0, keepdims=True) for f in range(3)
    ]
    filled = group > 0.5
    key = jnp.where(filled, group * STEP + high * 256.0 + low, EMPTY)
    floor = jnp.where(filled, group * STEP, NOBODY)
    eye = iota((total, total), 0) == iota((total, total), 1)
    key_col = jnp.sum(jnp.where(eye, key, 0.0), axis=1, keepdims=True)
    diagonal = jnp.where(eye, gram, 0.0)
    scale = lax.rsqrt(jnp.sum(diagonal, axis=0, keepdims=True) / width + 1e-06)
    scale_col = lax.rsqrt(jnp.sum(diagonal, axis=1, keepdims=True) / width + 1e-06)
    usable = (key_col < key) & (key_col >= floor)
    largest = jnp.max(jnp.where(usable, gram * scale_col, LOWEST), axis=0, keepdims=True)
    best = jnp.where(largest > LOWEST, jnp.maximum(largest * scale / width, -1.0), -1.0)
    for peer in range(peers):
        best_ref[peer] = best


def take_kernel(rows, me_ref, best_ref, route_ref, out_ref):
    peers, _, total = best_ref.shape
    count = out_ref.shape[1]
    dest = route_ref[0:1, :]
    slot = me_ref[0] * rows + route_ref[1:2, :]
    best = best_ref[:, 0, :]
    high = best.astype(jnp.bfloat16)
    rest = best - high.astype(jnp.float32)
    mid = rest.astype(jnp.bfloat16)
    low = (rest - mid.astype(jnp.float32)).astype(jnp.bfloat16)
    pick = (iota((total, count), 0) == slot).astype(jnp.bfloat16)
    found = nn(high, pick) + nn(mid, pick) + nn(low, pick)
    mine = iota((peers, count), 0) == dest
    out_ref[...] = jnp.sum(jnp.where(mine, found, 0.0), axis=0, keepdims=True)


def exchange(blocks):
    peers = blocks.shape[0]
    group = [(k + peers // 2 + 3) % peers for k in range(peers)]
    return lax.all_to_all(blocks, "owner", split_axis=0, concat_axis=0, tiled=True, axis_index_groups=[group])


def place_in_group():
    peers = lax.axis_size("owner")
    return ((lax.axis_index("owner") + (peers - peers // 2 - 3)) % peers).astype(jnp.int32).reshape(1)


def send(rows, cap, spread_out, embeds, cluster, order):
    count, width = embeds.shape
    peers = lax.axis_size("owner")
    total = peers * rows
    vmem = pl.BlockSpec(memory_space=pltpu.VMEM)
    smem = pl.BlockSpec(memory_space=pltpu.SMEM)
    packed, route = pl.pallas_call(
        functools.partial(pack_kernel, peers, rows, cap, spread_out),
        out_shape=[
            jax.ShapeDtypeStruct((total, width), jnp.bfloat16),
            jax.ShapeDtypeStruct((2, count), jnp.int32),
        ],
        in_specs=[pl.BlockSpec(memory_space=pl.ANY)] * 3,
        out_specs=[vmem] * 2,
        scratch_shapes=[
            pltpu.VMEM((1, count), jnp.int32),
            pltpu.VMEM((1, count), jnp.int32),
            pltpu.VMEM((count, width), jnp.bfloat16),
            pltpu.SemaphoreType.DMA((3,)),
        ],
        compiler_params=PARAMS,
    )(cluster.reshape(1, count), order.reshape(1, count), embeds)
    arrived = exchange(packed.reshape(peers, rows, width))
    best, crowded = pl.pallas_call(
        functools.partial(best_kernel, peers, rows, cap),
        out_shape=[jax.ShapeDtypeStruct((peers, 1, total), jnp.float32), jax.ShapeDtypeStruct((1,), jnp.int32)],
        in_specs=[vmem],
        out_specs=[vmem, smem],
        compiler_params=PARAMS,
    )(arrived.reshape(total, width))
    return best, route, crowded


def take(rows, me, returned, route):
    count = route.shape[1]
    vmem = pl.BlockSpec(memory_space=pltpu.VMEM)
    smem = pl.BlockSpec(memory_space=pltpu.SMEM)
    nearest = pl.pallas_call(
        functools.partial(take_kernel, rows),
        out_shape=jax.ShapeDtypeStruct((1, count), jnp.float32),
        in_specs=[smem, vmem, vmem],
        out_specs=vmem,
        compiler_params=PARAMS,
    )(me, returned, route)
    return nearest.reshape(count)


def per_device(embeds, cluster, order):
    count = embeds.shape[0]
    most = 2 * count // lax.axis_size("owner")

    def roomy():
        rows = -(-(most + 1) // 8) * 8
        best, route, _ = send(rows, most, False, embeds, cluster, order)
        return take(rows, place_in_group(), exchange(best), route)

    rows = 3 * most // 4
    if rows % 8:
        return roomy()
    best, route, crowded = send(rows, rows - 1, True, embeds, cluster, order)
    returned = exchange(best)

    def again():
        results = jnp.zeros_like(returned).at[0, 0, :count].set(roomy())
        places = jnp.stack([jnp.zeros((count,), jnp.int32), jnp.arange(count, dtype=jnp.int32)])
        return jnp.zeros((1,), jnp.int32), results, places

    return take(rows, *lax.cond(crowded[0] > 0, again, lambda: (place_in_group(), returned, route)))


def solution(mesh):
    placed = (P(("parts", "owner"), None), P(("parts", "owner")), P(("parts", "owner")))
    return jax.shard_map(
        per_device, mesh=mesh, in_specs=placed, out_specs=P(("parts", "owner")), check_vma=False
    )
```

```python
import functools

import jax
import jax.numpy as jnp
from jax import lax
from jax.experimental import pallas as pl
from jax.experimental.pallas import tpu as pltpu
from jax.sharding import PartitionSpec as P

CL_DEV = 4
LANES = 128
EMPTY = 1e9
NOBODY = 2e9
LOWEST = -3e38
STEP = 65536.0
PARAMS = pltpu.CompilerParams(vmem_limit_bytes=48 * 2**20)


def iota(shape, dim):
    return lax.broadcasted_iota(jnp.int32, shape, dim)


def nt(a, b):
    return lax.dot_general(a, b, (((1,), (1,)), ((), ())), preferred_element_type=jnp.float32)


def nn(a, b):
    return lax.dot_general(a, b, (((1,), (0,)), ((), ())), preferred_element_type=jnp.float32)


def parts(values):
    high = values.astype(jnp.bfloat16)
    rest = values - high.astype(jnp.float32)
    mid = rest.astype(jnp.bfloat16)
    low = (rest - mid.astype(jnp.float32)).astype(jnp.bfloat16)
    return jnp.concatenate([high, mid, low], axis=0)


def whole(sums):
    third = sums.shape[0] // 3
    return sums[:third] + sums[third:2 * third] + sums[2 * third:]


def pack_kernel(peers, rows, cap, spread_out, cl_hbm, od_hbm, x_hbm, out_ref, route_ref, cl_ref, od_ref, x_ref, sems):
    count, width = x_ref.shape
    step = 2 * LANES
    pieces = [(cl_hbm, cl_ref), (od_hbm, od_ref), (x_hbm, x_ref)]
    copies = [pltpu.make_async_copy(src, dst, sems.at[k]) for k, (src, dst) in enumerate(pieces)]
    for copy in copies:
        copy.start()
    before = (iota((count, count), 0) < iota((count, count), 1)).astype(jnp.bfloat16)
    tag_row = (iota((peers * rows, peers), 0) == iota((peers * rows, peers), 1) * rows + cap).astype(jnp.bfloat16)
    copies[0].wait()
    copies[1].wait()
    cl = cl_ref[...]
    od = od_ref[...]
    if spread_out:
        dest = cl & (peers - 1)
        group = cl >> (peers.bit_length() - 1)
    else:
        dest = cl >> (CL_DEV.bit_length() - 1)
        group = cl & (CL_DEV - 1)
    mine = iota((peers, count), 0) == dest
    ahead = nn(mine.astype(jnp.bfloat16), before)
    rank = jnp.sum(jnp.where(mine, ahead, 0.0), axis=0, keepdims=True).astype(jnp.int32)
    route_ref[0:1, :] = dest
    route_ref[1:2, :] = rank
    fits = rank < cap
    slot = jnp.where(fits, dest * rows + rank, -1)
    pick = (iota((peers * rows, count), 0) == slot).astype(jnp.bfloat16)
    fields = [od >> 8, od & 255, group + 1]
    spread = jnp.concatenate(
        [jnp.where(mine, f.astype(jnp.float32), 0.0) for f in fields], axis=0
    ).astype(jnp.bfloat16)
    place = ((iota((LANES, count), 0) == rank) & fits).astype(jnp.bfloat16)
    tags = nt(spread, place).astype(jnp.bfloat16)
    crowded = jnp.max((rank >= cap).astype(jnp.float32), axis=1, keepdims=True)
    crowded = jnp.broadcast_to(crowded, (peers, LANES)).astype(jnp.bfloat16)
    copies[2].wait()
    for k in range(width // step):
        part = nn(pick, x_ref[:, k * step:(k + 1) * step])
        if k == 0:
            part += nn(tag_row, jnp.concatenate([tags[0:peers], tags[peers:2 * peers]], axis=1))
        if k == 1:
            part += nn(tag_row, jnp.concatenate([tags[2 * peers:], crowded], axis=1))
        out_ref[:, k * step:(k + 1) * step] = part.astype(jnp.bfloat16)


def best_kernel(peers, rows, cap, x_ref, best_ref, crowded_ref):
    total, width = x_ref.shape
    gram = nt(x_ref[...], x_ref[...])
    tag_row = (iota((peers, total), 1) == iota((peers, total), 0) * rows + cap).astype(jnp.bfloat16)
    tags = nn(tag_row, x_ref[:, :4 * LANES])
    crowded_ref[0] = jnp.max(tags[:, 3 * LANES:]).astype(jnp.int32)
    cols = iota((peers, total), 1)
    first = iota((peers, total), 0) * rows
    block = (cols >= first) & (cols < first + rows)
    position = jnp.sum(jnp.where(block, cols - first, 0), axis=0, keepdims=True)
    spread = (iota((LANES, total), 0) == position).astype(jnp.bfloat16)
    fields = jnp.concatenate([tags[:, f * LANES:(f + 1) * LANES] for f in range(3)], axis=0).astype(jnp.bfloat16)
    flat = nn(fields, spread)
    high, low, group = [
        jnp.sum(jnp.where(block, flat[f * peers:(f + 1) * peers], 0.0), axis=0, keepdims=True) for f in range(3)
    ]
    filled = group > 0.5
    key = jnp.where(filled, group * STEP + high * 256.0 + low, EMPTY)
    floor = jnp.where(filled, group * STEP, NOBODY)
    eye = iota((total, total), 0) == iota((total, total), 1)
    key_col = jnp.sum(jnp.where(eye, key, 0.0), axis=1, keepdims=True)
    diagonal = jnp.where(eye, gram, 0.0)
    scale = lax.rsqrt(jnp.sum(diagonal, axis=0, keepdims=True) / width + 1e-06)
    scale_col = lax.rsqrt(jnp.sum(diagonal, axis=1, keepdims=True) / width + 1e-06)
    usable = (key_col < key) & (key_col >= floor)
    largest = jnp.max(jnp.where(usable, gram * scale_col, LOWEST), axis=0, keepdims=True)
    best = jnp.where(largest > LOWEST, jnp.maximum(largest * scale / width, -1.0), -1.0)
    shares = nt(parts(jnp.where(block, best, 0.0)), spread)
    best_ref[:, 0, :] = whole(shares)


def take_kernel(best_ref, route_ref, out_ref):
    peers, _, most = best_ref.shape
    count = out_ref.shape[1]
    pick = (iota((most, count), 0) == route_ref[1:2, :]).astype(jnp.bfloat16)
    found = whole(nn(parts(best_ref[:, 0, :]), pick))
    mine = iota((peers, count), 0) == route_ref[0:1, :]
    out_ref[...] = jnp.sum(jnp.where(mine, found, 0.0), axis=0, keepdims=True)


def exchange(blocks):
    peers = blocks.shape[0]
    group = [(k + peers // 2 + 3) % peers for k in range(peers)]
    return lax.all_to_all(blocks, "owner", split_axis=0, concat_axis=0, tiled=True, axis_index_groups=[group])


def send(rows, cap, spread_out, embeds, cluster, order):
    count, width = embeds.shape
    peers = lax.axis_size("owner")
    total = peers * rows
    vmem = pl.BlockSpec(memory_space=pltpu.VMEM)
    smem = pl.BlockSpec(memory_space=pltpu.SMEM)
    packed, route = pl.pallas_call(
        functools.partial(pack_kernel, peers, rows, cap, spread_out),
        out_shape=[
            jax.ShapeDtypeStruct((total, width), jnp.bfloat16),
            jax.ShapeDtypeStruct((2, count), jnp.int32),
        ],
        in_specs=[pl.BlockSpec(memory_space=pl.ANY)] * 3,
        out_specs=[vmem] * 2,
        scratch_shapes=[
            pltpu.VMEM((1, count), jnp.int32),
            pltpu.VMEM((1, count), jnp.int32),
            pltpu.VMEM((count, width), jnp.bfloat16),
            pltpu.SemaphoreType.DMA((3,)),
        ],
        compiler_params=PARAMS,
    )(cluster.reshape(1, count), order.reshape(1, count), embeds)
    arrived = exchange(packed.reshape(peers, rows, width))
    best, crowded = pl.pallas_call(
        functools.partial(best_kernel, peers, rows, cap),
        out_shape=[jax.ShapeDtypeStruct((peers, 1, LANES), jnp.float32), jax.ShapeDtypeStruct((1,), jnp.int32)],
        in_specs=[vmem],
        out_specs=[vmem, smem],
        compiler_params=PARAMS,
    )(arrived.reshape(total, width))
    return best, route, crowded


def take(returned, route):
    count = route.shape[1]
    vmem = pl.BlockSpec(memory_space=pltpu.VMEM)
    nearest = pl.pallas_call(
        take_kernel,
        out_shape=jax.ShapeDtypeStruct((1, count), jnp.float32),
        in_specs=[vmem] * 2,
        out_specs=vmem,
        compiler_params=PARAMS,
    )(returned, route)
    return nearest.reshape(count)


def per_device(embeds, cluster, order):
    count = embeds.shape[0]
    most = 2 * count // lax.axis_size("owner")

    def roomy():
        rows = -(-(most + 1) // 8) * 8
        best, route, _ = send(rows, most, False, embeds, cluster, order)
        return take(exchange(best), route)

    rows = 3 * most // 4
    if rows % 8:
        return roomy()
    best, route, crowded = send(rows, rows - 1, True, embeds, cluster, order)
    returned = exchange(best)

    def again():
        table = roomy().reshape(-1, LANES)
        results = jnp.zeros_like(returned).at[: table.shape[0], 0].set(table)
        row = jnp.arange(count, dtype=jnp.int32)
        return results, jnp.stack([row // LANES, row % LANES])

    return take(*lax.cond(crowded[0] > 0, again, lambda: (returned, route)))


def solution(mesh):
    placed = (P(("parts", "owner"), None), P(("parts", "owner")), P(("parts", "owner")))
    return jax.shard_map(
        per_device, mesh=mesh, in_specs=placed, out_specs=P(("parts", "owner")), check_vma=False
    )
```

```python
import functools

import jax
import jax.numpy as jnp
from jax import lax
from jax.experimental import pallas as pl
from jax.experimental.pallas import tpu as pltpu
from jax.sharding import PartitionSpec as P

CL_DEV = 4
LANES = 128
EMPTY = 1e9
NOBODY = 2e9
LOWEST = -3e38
STEP = 65536.0
PARAMS = pltpu.CompilerParams(vmem_limit_bytes=48 * 2**20)


def iota(shape, dim):
    return lax.broadcasted_iota(jnp.int32, shape, dim)


def nt(a, b):
    return lax.dot_general(a, b, (((1,), (1,)), ((), ())), preferred_element_type=jnp.float32)


def nn(a, b):
    return lax.dot_general(a, b, (((1,), (0,)), ((), ())), preferred_element_type=jnp.float32)


def parts(values):
    high = values.astype(jnp.bfloat16)
    rest = values - high.astype(jnp.float32)
    mid = rest.astype(jnp.bfloat16)
    low = (rest - mid.astype(jnp.float32)).astype(jnp.bfloat16)
    return jnp.concatenate([high, mid, low], axis=0)


def whole(sums):
    third = sums.shape[0] // 3
    return sums[:third] + sums[third:2 * third] + sums[2 * third:]


def pack_kernel(peers, rows, cap, spread_out, cl_hbm, od_hbm, x_hbm, out_ref, route_ref, cl_ref, od_ref, x_ref, sems):
    count, width = x_ref.shape
    step = 2 * LANES
    pieces = [(cl_hbm, cl_ref), (od_hbm, od_ref), (x_hbm, x_ref)]
    copies = [pltpu.make_async_copy(src, dst, sems.at[k]) for k, (src, dst) in enumerate(pieces)]
    for copy in copies:
        copy.start()
    before = (iota((count, count), 0) < iota((count, count), 1)).astype(jnp.bfloat16)
    tag_row = (iota((peers * rows, peers), 0) == iota((peers * rows, peers), 1) * rows + cap).astype(jnp.bfloat16)
    copies[0].wait()
    copies[1].wait()
    cl = cl_ref[...]
    od = od_ref[...]
    if spread_out:
        dest = cl & (peers - 1)
        group = cl >> (peers.bit_length() - 1)
    else:
        dest = cl >> (CL_DEV.bit_length() - 1)
        group = cl & (CL_DEV - 1)
    mine = iota((peers, count), 0) == dest
    ahead = nn(mine.astype(jnp.bfloat16), before)
    rank = jnp.sum(jnp.where(mine, ahead, 0.0), axis=0, keepdims=True).astype(jnp.int32)
    route_ref[0:1, :] = dest
    route_ref[1:2, :] = rank
    fits = rank < cap
    slot = jnp.where(fits, dest * rows + rank, -1)
    pick = (iota((peers * rows, count), 0) == slot).astype(jnp.bfloat16)
    fields = [od >> 8, od & 255, group + 1]
    spread = jnp.concatenate(
        [jnp.where(mine, f.astype(jnp.float32), 0.0) for f in fields], axis=0
    ).astype(jnp.bfloat16)
    place = ((iota((LANES, count), 0) == rank) & fits).astype(jnp.bfloat16)
    tags = nt(spread, place).astype(jnp.bfloat16)
    crowded = jnp.max((rank >= cap).astype(jnp.float32), axis=1, keepdims=True)
    crowded = jnp.broadcast_to(crowded, (peers, LANES)).astype(jnp.bfloat16)
    copies[2].wait()
    for k in reversed(range(width // step)):
        part = nn(pick, x_ref[:, k * step:(k + 1) * step])
        if k == 0:
            part += nn(tag_row, jnp.concatenate([tags[0:peers], tags[peers:2 * peers]], axis=1))
        if k == 1:
            part += nn(tag_row, jnp.concatenate([tags[2 * peers:], crowded], axis=1))
        out_ref[:, k * step:(k + 1) * step] = part.astype(jnp.bfloat16)


def best_kernel(peers, rows, cap, x_ref, best_ref, crowded_ref):
    total, width = x_ref.shape
    gram = nt(x_ref[...], x_ref[...])
    tag_row = (iota((peers, total), 1) == iota((peers, total), 0) * rows + cap).astype(jnp.bfloat16)
    tags = nn(tag_row, x_ref[:, :4 * LANES])
    crowded_ref[...] = jnp.max(tags[:, 3 * LANES:], axis=0, keepdims=True)
    cols = iota((peers, total), 1)
    first = iota((peers, total), 0) * rows
    block = (cols >= first) & (cols < first + rows)
    position = jnp.sum(jnp.where(block, cols - first, 0), axis=0, keepdims=True)
    spread = (iota((LANES, total), 0) == position).astype(jnp.bfloat16)
    fields = jnp.concatenate([tags[:, f * LANES:(f + 1) * LANES] for f in range(3)], axis=0).astype(jnp.bfloat16)
    flat = nn(fields, spread)
    high, low, group = [
        jnp.sum(jnp.where(block, flat[f * peers:(f + 1) * peers], 0.0), axis=0, keepdims=True) for f in range(3)
    ]
    filled = group > 0.5
    key = jnp.where(filled, group * STEP + high * 256.0 + low, EMPTY)
    floor = jnp.where(filled, group * STEP, NOBODY)
    eye = iota((total, total), 0) == iota((total, total), 1)
    key_col = jnp.sum(jnp.where(eye, key, 0.0), axis=1, keepdims=True)
    diagonal = jnp.where(eye, gram, 0.0)
    scale = lax.rsqrt(jnp.sum(diagonal, axis=0, keepdims=True) / width + 1e-06)
    scale_col = lax.rsqrt(jnp.sum(diagonal, axis=1, keepdims=True) / width + 1e-06)
    usable = (key_col < key) & (key_col >= floor)
    largest = jnp.max(jnp.where(usable, gram * scale_col, LOWEST), axis=0, keepdims=True)
    best = jnp.where(largest > LOWEST, jnp.maximum(largest * scale / width, -1.0), -1.0)
    shares = nt(parts(jnp.where(block, best, 0.0)), spread)
    best_ref[:, 0, :] = whole(shares)


def take_kernel(best_ref, route_ref, out_ref):
    peers, _, most = best_ref.shape
    count = out_ref.shape[1]
    pick = (iota((most, count), 0) == route_ref[1:2, :]).astype(jnp.bfloat16)
    found = whole(nn(parts(best_ref[:, 0, :]), pick))
    mine = iota((peers, count), 0) == route_ref[0:1, :]
    out_ref[...] = jnp.sum(jnp.where(mine, found, 0.0), axis=0, keepdims=True)


def exchange(blocks):
    peers = blocks.shape[0]
    group = [k ^ (peers // 2 + 3) for k in range(peers)]
    return lax.all_to_all(blocks, "owner", split_axis=0, concat_axis=0, tiled=True, axis_index_groups=[group])


def send(rows, cap, spread_out, embeds, cluster, order):
    count, width = embeds.shape
    peers = lax.axis_size("owner")
    total = peers * rows
    vmem = pl.BlockSpec(memory_space=pltpu.VMEM)
    packed, route = pl.pallas_call(
        functools.partial(pack_kernel, peers, rows, cap, spread_out),
        out_shape=[
            jax.ShapeDtypeStruct((total, width), jnp.bfloat16),
            jax.ShapeDtypeStruct((2, count), jnp.int32),
        ],
        in_specs=[pl.BlockSpec(memory_space=pl.ANY)] * 3,
        out_specs=[vmem] * 2,
        scratch_shapes=[
            pltpu.VMEM((1, count), jnp.int32),
            pltpu.VMEM((1, count), jnp.int32),
            pltpu.VMEM((count, width), jnp.bfloat16),
            pltpu.SemaphoreType.DMA((3,)),
        ],
        compiler_params=PARAMS,
    )(cluster.reshape(1, count), order.reshape(1, count), embeds)
    arrived = exchange(packed.reshape(peers, rows, width))
    best, crowded = pl.pallas_call(
        functools.partial(best_kernel, peers, rows, cap),
        out_shape=[jax.ShapeDtypeStruct((peers, 1, LANES), jnp.float32), jax.ShapeDtypeStruct((1, LANES), jnp.float32)],
        in_specs=[vmem],
        out_specs=[vmem, vmem],
        compiler_params=PARAMS,
    )(arrived.reshape(total, width))
    return best, route, crowded


def take(returned, route):
    count = route.shape[1]
    vmem = pl.BlockSpec(memory_space=pltpu.VMEM)
    nearest = pl.pallas_call(
        take_kernel,
        out_shape=jax.ShapeDtypeStruct((1, count), jnp.float32),
        in_specs=[vmem] * 2,
        out_specs=vmem,
        compiler_params=PARAMS,
    )(returned, route)
    return nearest.reshape(count)


def per_device(embeds, cluster, order):
    count = embeds.shape[0]
    most = 2 * count // lax.axis_size("owner")

    def roomy():
        rows = -(-(most + 1) // 8) * 8
        best, route, _ = send(rows, most, False, embeds, cluster, order)
        return take(exchange(best), route)

    rows = 3 * most // 4
    if rows % 8:
        return roomy()
    best, route, crowded = send(rows, rows - 1, True, embeds, cluster, order)
    returned = exchange(best)

    def again():
        table = roomy().reshape(-1, LANES)
        results = jnp.zeros_like(returned).at[: table.shape[0], 0].set(table)
        row = jnp.arange(count, dtype=jnp.int32)
        return results, jnp.stack([row // LANES, row % LANES])

    return take(*lax.cond(crowded[0, 0] > 0, again, lambda: (returned, route)))


def solution(mesh):
    placed = (P(("parts", "owner"), None), P(("parts", "owner")), P(("parts", "owner")))
    return jax.shard_map(
        per_device, mesh=mesh, in_specs=placed, out_specs=P(("parts", "owner")), check_vma=False
    )
```

```python
import functools

import jax
import jax.numpy as jnp
from jax import lax
from jax.experimental import pallas as pl
from jax.experimental.pallas import tpu as pltpu
from jax.sharding import PartitionSpec as P

CL_DEV = 4
LANES = 128
EMPTY = 1e9
NOBODY = 2e9
LOWEST = -3e38
STEP = 65536.0
PARAMS = pltpu.CompilerParams(vmem_limit_bytes=48 * 2**20)


def iota(shape, dim):
    return lax.broadcasted_iota(jnp.int32, shape, dim)


def nt(a, b):
    return lax.dot_general(a, b, (((1,), (1,)), ((), ())), preferred_element_type=jnp.float32)


def nn(a, b):
    return lax.dot_general(a, b, (((1,), (0,)), ((), ())), preferred_element_type=jnp.float32)


def parts(values):
    high = values.astype(jnp.bfloat16)
    rest = values - high.astype(jnp.float32)
    mid = rest.astype(jnp.bfloat16)
    low = (rest - mid.astype(jnp.float32)).astype(jnp.bfloat16)
    return jnp.concatenate([high, mid, low], axis=0)


def whole(sums):
    third = sums.shape[0] // 3
    return sums[:third] + sums[third:2 * third] + sums[2 * third:]


def pack_kernel(peers, rows, cap, spread_out, cl_hbm, od_hbm, x_hbm, out_ref, route_ref, cl_ref, od_ref, x_ref, sems):
    count, width = x_ref.shape
    step = 4 * LANES
    pieces = [(cl_hbm, cl_ref), (od_hbm, od_ref), (x_hbm, x_ref)]
    copies = [pltpu.make_async_copy(src, dst, sems.at[k]) for k, (src, dst) in enumerate(pieces)]
    for copy in copies:
        copy.start()
    before = (iota((count, count), 0) < iota((count, count), 1)).astype(jnp.bfloat16)
    tag_row = (iota((peers * rows, peers), 0) == iota((peers * rows, peers), 1) * rows + cap).astype(jnp.bfloat16)
    copies[0].wait()
    copies[1].wait()
    cl = cl_ref[...]
    od = od_ref[...]
    if spread_out:
        dest = cl & (peers - 1)
        group = cl >> (peers.bit_length() - 1)
    else:
        dest = cl >> (CL_DEV.bit_length() - 1)
        group = cl & (CL_DEV - 1)
    mine = iota((peers, count), 0) == dest
    ahead = nn(mine.astype(jnp.bfloat16), before)
    rank = jnp.sum(jnp.where(mine, ahead, 0.0), axis=0, keepdims=True).astype(jnp.int32)
    route_ref[0:1, :] = dest
    route_ref[1:2, :] = rank
    fits = rank < cap
    slot = jnp.where(fits, dest * rows + rank, -1)
    pick = (iota((peers * rows, count), 0) == slot).astype(jnp.bfloat16)
    fields = [od >> 8, od & 255, group + 1]
    spread = jnp.concatenate(
        [jnp.where(mine, f.astype(jnp.float32), 0.0) for f in fields], axis=0
    ).astype(jnp.bfloat16)
    place = ((iota((LANES, count), 0) == rank) & fits).astype(jnp.bfloat16)
    tags = nt(spread, place).astype(jnp.bfloat16)
    crowded = jnp.max((rank >= cap).astype(jnp.float32), axis=1, keepdims=True)
    crowded = jnp.broadcast_to(crowded, (peers, LANES)).astype(jnp.bfloat16)
    copies[2].wait()
    for k in reversed(range(width // step)):
        part = nn(pick, x_ref[:, k * step:(k + 1) * step])
        if k == 0:
            fields = [tags[f * peers:(f + 1) * peers] for f in range(3)]
            part += nn(tag_row, jnp.concatenate([*fields, crowded], axis=1))
        out_ref[:, k * step:(k + 1) * step] = part.astype(jnp.bfloat16)


def best_kernel(peers, rows, cap, x_ref, best_ref, crowded_ref):
    total, width = x_ref.shape
    gram = nt(x_ref[...], x_ref[...])
    tag_row = (iota((peers, total), 1) == iota((peers, total), 0) * rows + cap).astype(jnp.bfloat16)
    tags = nn(tag_row, x_ref[:, :4 * LANES])
    crowded_ref[...] = jnp.max(tags[:, 3 * LANES:], axis=0, keepdims=True)
    cols = iota((peers, total), 1)
    first = iota((peers, total), 0) * rows
    block = (cols >= first) & (cols < first + rows)
    position = jnp.sum(jnp.where(block, cols - first, 0), axis=0, keepdims=True)
    spread = (iota((LANES, total), 0) == position).astype(jnp.bfloat16)
    fields = jnp.concatenate([tags[:, f * LANES:(f + 1) * LANES] for f in range(3)], axis=0).astype(jnp.bfloat16)
    flat = nn(fields, spread)
    high, low, group = [
        jnp.sum(jnp.where(block, flat[f * peers:(f + 1) * peers], 0.0), axis=0, keepdims=True) for f in range(3)
    ]
    filled = group > 0.5
    key = jnp.where(filled, group * STEP + high * 256.0 + low, EMPTY)
    floor = jnp.where(filled, group * STEP, NOBODY)
    eye = iota((total, total), 0) == iota((total, total), 1)
    key_col = jnp.sum(jnp.where(eye, key, 0.0), axis=1, keepdims=True)
    diagonal = jnp.where(eye, gram, 0.0)
    scale = lax.rsqrt(jnp.sum(diagonal, axis=0, keepdims=True) / width + 1e-06)
    scale_col = lax.rsqrt(jnp.sum(diagonal, axis=1, keepdims=True) / width + 1e-06)
    usable = (key_col < key) & (key_col >= floor)
    largest = jnp.max(jnp.where(usable, gram * scale_col, LOWEST), axis=0, keepdims=True)
    best = jnp.where(largest > LOWEST, jnp.maximum(largest * scale / width, -1.0), -1.0)
    shares = nt(parts(jnp.where(block, best, 0.0)), spread)
    best_ref[:, 0, :] = whole(shares)


def take_kernel(best_ref, route_ref, out_ref):
    peers, _, most = best_ref.shape
    count = out_ref.shape[1]
    pick = (iota((most, count), 0) == route_ref[1:2, :]).astype(jnp.bfloat16)
    found = whole(nn(parts(best_ref[:, 0, :]), pick))
    mine = iota((peers, count), 0) == route_ref[0:1, :]
    out_ref[...] = jnp.sum(jnp.where(mine, found, 0.0), axis=0, keepdims=True)


def exchange(blocks):
    peers = blocks.shape[0]
    group = [k ^ (peers // 2 + 3) for k in range(peers)]
    return lax.all_to_all(blocks, "owner", split_axis=0, concat_axis=0, tiled=True, axis_index_groups=[group])


def send(rows, cap, spread_out, embeds, cluster, order):
    count, width = embeds.shape
    peers = lax.axis_size("owner")
    total = peers * rows
    vmem = pl.BlockSpec(memory_space=pltpu.VMEM)
    packed, route = pl.pallas_call(
        functools.partial(pack_kernel, peers, rows, cap, spread_out),
        out_shape=[
            jax.ShapeDtypeStruct((total, width), jnp.bfloat16),
            jax.ShapeDtypeStruct((2, count), jnp.int32),
        ],
        in_specs=[pl.BlockSpec(memory_space=pl.ANY)] * 3,
        out_specs=[vmem] * 2,
        scratch_shapes=[
            pltpu.VMEM((1, count), jnp.int32),
            pltpu.VMEM((1, count), jnp.int32),
            pltpu.VMEM((count, width), jnp.bfloat16),
            pltpu.SemaphoreType.DMA((3,)),
        ],
        compiler_params=PARAMS,
    )(cluster.reshape(1, count), order.reshape(1, count), embeds)
    arrived = exchange(packed.reshape(peers, rows, width))
    best, crowded = pl.pallas_call(
        functools.partial(best_kernel, peers, rows, cap),
        out_shape=[jax.ShapeDtypeStruct((peers, 1, LANES), jnp.float32), jax.ShapeDtypeStruct((1, LANES), jnp.float32)],
        in_specs=[vmem],
        out_specs=[vmem, vmem],
        compiler_params=PARAMS,
    )(arrived.reshape(total, width))
    return best, route, crowded


def take(returned, route):
    count = route.shape[1]
    vmem = pl.BlockSpec(memory_space=pltpu.VMEM)
    nearest = pl.pallas_call(
        take_kernel,
        out_shape=jax.ShapeDtypeStruct((1, count), jnp.float32),
        in_specs=[vmem] * 2,
        out_specs=vmem,
        compiler_params=PARAMS,
    )(returned, route)
    return nearest.reshape(count)


def per_device(embeds, cluster, order):
    count = embeds.shape[0]
    most = 2 * count // lax.axis_size("owner")

    def roomy():
        rows = -(-(most + 1) // 8) * 8
        best, route, _ = send(rows, most, False, embeds, cluster, order)
        return take(exchange(best), route)

    rows = 3 * most // 4
    if rows % 8:
        return roomy()
    best, route, crowded = send(rows, rows - 1, True, embeds, cluster, order)
    returned = exchange(best)

    def again():
        table = roomy().reshape(-1, LANES)
        results = jnp.zeros_like(returned).at[: table.shape[0], 0].set(table)
        row = jnp.arange(count, dtype=jnp.int32)
        return results, jnp.stack([row // LANES, row % LANES])

    return take(*lax.cond(crowded[0, 0] > 0, again, lambda: (returned, route)))


def solution(mesh):
    placed = (P(("parts", "owner"), None), P(("parts", "owner")), P(("parts", "owner")))
    return jax.shard_map(
        per_device, mesh=mesh, in_specs=placed, out_specs=P(("parts", "owner")), check_vma=False
    )
```
